256 devices in a mesh: section: 16 (over z, core), expert: 16 (over x, y).
Axes of the slice: x: 4, y: 4, z: 8, core: 2. Of those that a mesh axis runs over, the one named last changes fastest.
Arguments:
- forward_in: bfloat16 [16, 1024, 3584], P('section', 'expert'), may hold values from -20 to 20
- reverse_in: bfloat16 [16, 1024, 3584], P('section', 'expert'), may hold values from -20 to 20
- w_gate: bfloat16 [16, 3584, 8192], P('section', None, 'expert'), may hold values from -0.09375 to 0.09375
- w_up: bfloat16 [16, 3584, 8192], P('section', None, 'expert'), may hold values from -0.09375 to 0.09375
- w_down: bfloat16 [16, 8192, 3584], P('section', 'expert'), may hold values from -0.1875 to 0.1875
- routes: int32 [16, 2, 16, 1024, 1], P('section', None, None, 'expert'), may hold values from 0 to 7; in each aligned block of 64 rows (0 to 63, 64 to 127, ..., all dimensions but the last counted through in order) at most 24 rows name the same one
- gate_weight: float32 [16, 2, 16, 1024], P('section', None, None, 'expert'), may hold values from 0.5 to 1.5
Outputs:
- forward_out: bfloat16 [16, 1024, 3584], P('section', 'expert')
- reverse_out: bfloat16 [16, 1024, 3584], P('section', 'expert')
The draws below stay inside these ranges and needn't reach their ends.
Inputs may be any that keep to these rules, and one draw needn't show every extreme that they name: `routes`: within each block of 64 tokens of one layer, direction and micro-batch, no expert is chosen more than 24 times, and in some of these blocks one expert is chosen exactly 24 times.
All inputs are finite; a program needn't handle non-finite values.
Results may differ from the reference program's by a relative error of at most 0.0067.
Values may be sent and summed in bfloat16 or wider, within the bound.
No kernel may reach another device: no remote copies, remote signals or barrier semaphores. Data moves between devices by JAX's collectives and lax.ppermute only.
A program may use at most 128 MiB of HBM per device.

```python
import math
import jax
import jax.numpy as jnp
import numpy as np
from jax import lax

D = 3584
HID = 1024
ROWS = 64
EXPERTS = 8
MOST = 24
TOKENS = 1024
TICKS = 2
N_SECTION = 16
N_EXPERT = 16


def scaled_field(key, base, row_low, row_high):
    row_key, col_key = jax.random.split(key)
    row_scale = jnp.exp(jax.random.uniform(row_key, (N_SECTION, TOKENS, 1), jnp.float32, math.log(row_low), math.log(row_high)))
    col_scale = jnp.exp(jax.random.uniform(col_key, (1, 1, D), jnp.float32, math.log(0.6), math.log(1.6)))
    return (base * row_scale * col_scale).astype(jnp.bfloat16)


def draw_forward_in(key, part):
    key = jax.random.fold_in(key, 11)
    base_key, scale_key = jax.random.split(key, 2)
    base = jnp.clip(jax.random.normal(base_key, (N_SECTION, TOKENS, D), jnp.float32), -4.0, 4.0)
    return scaled_field(scale_key, base, 0.3, 3.0)


def draw_reverse_in(key, part):
    key = jax.random.fold_in(key, 23)
    base_key, scale_key = jax.random.split(key, 2)
    base = jnp.clip(jax.random.normal(base_key, (N_SECTION, TOKENS, D), jnp.float32), -4.0, 4.0)
    return scaled_field(scale_key, base, 0.3, 3.0)


def block_scale(rng, dims, shards, smallest, high):
    def one(position, blocks):
        heights = jax.random.uniform(jax.random.fold_in(jax.random.fold_in(rng, 6), position), (blocks,), jnp.float32, smallest / len(shards), high / len(shards))
        return jnp.repeat(jnp.exp(heights), dims[position] // blocks).reshape((-1,) + (1,) * (len(dims) - position - 1))

    factor_of = one(*shards[0])
    for cut in shards[1:]:
        factor_of = factor_of * one(*cut)
    return factor_of


def shared_out(key, own, number, rows, count, top, bound, skew):
    sequence = jax.random.permutation(key, count)
    crowded, common = shares(count, rows * top, bound, skew, True), shares(count, rows * top, bound, skew, False)
    places = jnp.arange(count)

    def named(sizes, turn):
        used = int((sizes > 0).sum())
        fixed = max(1, used // 4)
        shifted = fixed + (places - fixed + turn * (used - fixed)) % max(1, count - fixed)
        return jnp.zeros((count,), jnp.int32).at[sequence[jnp.where(places < fixed, places, shifted)]].set(jnp.asarray(sizes, jnp.int32))

    sizes = jnp.where(number % 4 == 0, named(crowded, number // 4), named(common, number - number // 4 - 1))
    mixed = jax.random.permutation(jax.random.fold_in(own, 3), count)
    source_of, sink = mixed[0:count // 2 * 2:2], mixed[1:count // 2 * 2:2]
    margin = jnp.minimum(sizes[source_of] - 1, bound - sizes[sink]) // 2
    margin = jnp.where((source_of == sequence[0]) | (sink == sequence[0]) | (sizes[sink] == 0), 0, jnp.maximum(margin, 0))
    shifted = jax.random.randint(jax.random.fold_in(own, 4), (count // 2,), 0, 1 << 20) % (margin + 1)
    sizes = sizes.at[source_of].add(-shifted).at[sink].add(shifted)
    labels = jnp.searchsorted(jnp.cumsum(sizes), jnp.arange(rows * top), side="right").astype(jnp.int32)
    grid = labels.reshape(top, rows).T
    grid = grid[jax.random.permutation(jax.random.fold_in(own, 1), rows)]
    turn = jax.random.randint(jax.random.fold_in(own, 2), (rows, 1), 0, top)
    return jnp.take_along_axis(grid, (jnp.arange(top)[None, :] + turn) % top, axis=1)


def shares(number_of, total, limit, skew, full):
    loads = [(1 << 20) // math.isqrt(grade ** skew) + 1 for grade in range(1, number_of + 1)]
    largest = limit if full else min(limit, max(-(-total // number_of), total * loads[0] // sum(loads)))
    least = 1 if total - largest >= number_of - 1 else 0
    given, spare = [largest] + [least] * (number_of - 1), total - largest - least * (number_of - 1)
    while spare > 0:
        free = [i for i in range(1, number_of) if given[i] < largest] or [i for i in range(1, number_of) if given[i] < limit]
        pool, budget = sum([loads[i] for i in free]), spare
        for i in free:
            extra = min(limit - given[i], max(1, budget * loads[i] // pool), spare)
            given[i] = given[i] + extra
            spare = spare - extra
    return np.array(given)


def centred(own_key, extent, deviation, bound, pieces=(), kind=jnp.bfloat16):
    entries = deviation * jax.random.normal(own_key, extent, jnp.float32)
    if pieces:
        entries = entries * block_scale(own_key, extent, pieces, -0.22, 0.18)
    return jnp.clip(entries, -bound, bound).astype(kind)


def setup_inputs(seed: int = 0) -> dict:
    splits = jax.random.split(jax.random.key(seed), 8)
    forward_in = draw_forward_in(jax.random.fold_in(splits[7], 71), 0)
    reverse_in = draw_reverse_in(jax.random.fold_in(splits[7], 71), 0)
    w_gate = centred(splits[2], (N_SECTION, D, EXPERTS * HID), D ** -0.5, 0.09375, ((0, 16), (2, 16)))
    w_up = centred(splits[3], (N_SECTION, D, EXPERTS * HID), D ** -0.5, 0.09375, ((0, 16), (2, 16)))
    w_down = centred(splits[4], (N_SECTION, EXPERTS * HID, D), HID ** -0.5, 0.1875, ((0, 16), (1, 16)))
    routes_keys = jax.random.split(jax.random.fold_in(splits[5], 1), N_SECTION * 2 * N_SECTION * TOKENS // ROWS)
    routes_turns = jax.random.permutation(jax.random.fold_in(splits[5], 3), N_SECTION * 2 * N_SECTION * TOKENS // ROWS)
    routes = jax.vmap(lambda own, number: shared_out(jax.random.fold_in(splits[5], 2), own, number, ROWS, EXPERTS, 1, MOST, 2))(routes_keys, routes_turns).reshape((N_SECTION, 2, N_SECTION, TOKENS, 1))
    gate_weight = jnp.clip(0.5 + 1.0 * jax.random.uniform(splits[6], (N_SECTION, 2, N_SECTION, TOKENS), jnp.float32) ** block_scale(splits[6], (N_SECTION, 2, N_SECTION, TOKENS), ((0, 16), (3, 16)), -0.2, 0.2), 0.5, 1.5)
    return dict(forward_in=forward_in, reverse_in=reverse_in, w_gate=w_gate, w_up=w_up, w_down=w_down, routes=routes, gate_weight=gate_weight)


epsilon = 1e-06

def normalize(token_rows):
    widened = token_rows.astype(jnp.float32)
    inverse = lax.rsqrt(lax.optimization_barrier(jnp.mean(widened * widened, axis=-1, keepdims=True)) + epsilon)
    return (widened * inverse).astype(jnp.bfloat16)

def expert_rows(packed, gate_cols, up_cols, down_rows):
    gate_out = jnp.dot(packed, gate_cols, preferred_element_type=jnp.float32)
    up_out = jnp.dot(packed, up_cols, preferred_element_type=jnp.float32)
    active = (jax.nn.silu(gate_out) * up_out).astype(jnp.bfloat16)
    half_hid = HID // 2
    low_part = jnp.dot(active[:, :half_hid], down_rows[:half_hid], preferred_element_type=jnp.float32).astype(jnp.bfloat16)
    high_part = jnp.dot(active[:, half_hid:], down_rows[half_hid:], preferred_element_type=jnp.float32).astype(jnp.bfloat16)
    return (low_part.astype(jnp.float32) + high_part.astype(jnp.float32)).astype(jnp.bfloat16)

def apply_layer(current, gate_layer, up_layer, down_layer, chosen_flat, weights):
    normed = normalize(current)
    chosen = chosen_flat.reshape(N_EXPERT, ROWS)
    onehot = (chosen[:, :, None] == jnp.arange(EXPERTS, dtype=jnp.int32)[None, None, :]).astype(jnp.int32)
    ranked = lax.optimization_barrier(jnp.sum((jnp.cumsum(onehot, axis=1) - onehot) * onehot, axis=2))
    source = jnp.arange(N_EXPERT, dtype=jnp.int32)[:, None]
    slot_of = ((chosen * N_EXPERT + source) * MOST + ranked).reshape(-1)
    slot_count = N_EXPERT * MOST
    buffer = jnp.zeros((EXPERTS * slot_count, D), jnp.bfloat16).at[slot_of].set(normed)
    buffer = buffer.reshape(EXPERTS, slot_count, D)

    def per_expert(expert):
        packed = lax.dynamic_index_in_dim(buffer, expert, 0, keepdims=False)
        gate_cols = lax.dynamic_slice_in_dim(gate_layer, expert * HID, HID, 1)
        up_cols = lax.dynamic_slice_in_dim(up_layer, expert * HID, HID, 1)
        down_rows = lax.dynamic_slice_in_dim(down_layer, expert * HID, HID, 0)
        return expert_rows(packed, gate_cols, up_cols, down_rows)
    outputs = lax.map(per_expert, jnp.arange(EXPERTS, dtype=jnp.int32))
    picked = jnp.take(outputs.reshape(EXPERTS * slot_count, D), slot_of, axis=0)
    return (current.astype(jnp.float32) + weights[:, None] * picked.astype(jnp.float32)).astype(jnp.bfloat16)

def run_direction(states, heading, direction, w_gate, w_up, w_down, routes, gate_weight):

    def one_batch(batch_index):
        initial = states[batch_index]

        def advance(tick_index, current):
            layer_index = batch_index + heading * tick_index
            is_live = jnp.logical_and(layer_index >= 0, layer_index <= N_SECTION - 1)
            clamped = jnp.clip(layer_index, 0, N_SECTION - 1)

            def apply_now(value):
                return apply_layer(value, w_gate[clamped], w_up[clamped], w_down[clamped], routes[clamped, direction, batch_index, :, 0], gate_weight[clamped, direction, batch_index])

            def keep_same(value):
                return value
            return lax.cond(is_live, apply_now, keep_same, current)
        return lax.fori_loop(0, TICKS, advance, initial)
    return lax.map(one_batch, jnp.arange(N_SECTION, dtype=jnp.int32))

def reference(forward_in, reverse_in, w_gate, w_up, w_down, routes, gate_weight):
    forward_done = run_direction(forward_in, 1, 0, w_gate, w_up, w_down, routes, gate_weight)
    reverse_done = run_direction(reverse_in, -1, 1, w_gate, w_up, w_down, routes, gate_weight)
    return (jnp.roll(forward_done, TICKS, axis=0), jnp.roll(reverse_done, -TICKS, axis=0))
```

```python
import jax
import jax.numpy as jnp
from jax import lax
from jax.experimental import pallas as pl
from jax.experimental.pallas import tpu as pltpu
from jax.sharding import PartitionSpec as P

epsilon = 1e-06
MIB = 1 << 20


def together(*arrays):
    return lax.optimization_barrier(arrays)


def bits(mask):
    return mask.astype(jnp.float32).astype(jnp.bfloat16)


def normed_select(slots, parts, slot_total):
    widened = [part.astype(jnp.float32) for part in parts]
    total = sum(jnp.sum(part * part, axis=-1, keepdims=True) for part in widened)
    width = sum(part.shape[1] for part in parts)
    inverse = lax.rsqrt(total / width + epsilon)
    select = bits(lax.broadcasted_iota(jnp.int32, (slot_total, slots.shape[1]), 0) == slots)
    packed = []
    for part in widened:
        normed = (part * inverse).astype(jnp.bfloat16)
        rows = jnp.dot(select, normed, preferred_element_type=jnp.float32)
        packed.append(rows.astype(jnp.bfloat16))
    return packed


def first_pack_kernel(slots_ref, own_ref, mate_ref, out_ref):
    rows = jnp.concatenate([own_ref[...], mate_ref[...]], axis=0)
    out_ref[...] = normed_select(slots_ref[...], [rows], out_ref.shape[0])[0]


def pack_kernel(group_ref, slots_ref, near_ref, far_ref, out_ref):
    near, far = near_ref[...], far_ref[...]
    half = near.shape[1]
    count = far.shape[0] // 2
    far = jnp.concatenate([far[count:], far[:count]], axis=0)
    first = group_ref[...] == 0
    parts = [jnp.where(first, near, far), jnp.where(first, far, near)]
    low, high = normed_select(slots_ref[...], parts, out_ref.shape[0])
    out_ref[:, :half] = low
    out_ref[:, half:] = high


def pack(kernel, slot_total, features, *operands):
    rows = 128
    return pl.pallas_call(
        kernel,
        out_shape=jax.ShapeDtypeStruct((slot_total, features), jnp.bfloat16),
        compiler_params=pltpu.CompilerParams(vmem_limit_bytes=32 * MIB),
        cost_estimate=pl.CostEstimate(
            flops=2 * slot_total * rows * features,
            bytes_accessed=2 * (slot_total + rows) * features,
            transcendentals=0,
        ),
    )(*operands)


def hidden_kernel(rows_ref, gate_ref, up_ref, out_ref):
    rows = rows_ref[...]
    gate_out = jnp.dot(rows, gate_ref[...], preferred_element_type=jnp.float32)
    up_out = jnp.dot(rows, up_ref[...], preferred_element_type=jnp.float32)
    out_ref[...] = (gate_out / (1.0 + jnp.exp(-gate_out)) * up_out).astype(jnp.bfloat16)


def hidden(rows, gate_cols, up_cols):
    count, features = rows.shape
    width = gate_cols.shape[1]
    block = min(256, width)
    return pl.pallas_call(
        hidden_kernel,
        grid=(width // block,),
        in_specs=[
            pl.BlockSpec((count, features), lambda j: (0, 0)),
            pl.BlockSpec((features, block), lambda j: (0, j)),
            pl.BlockSpec((features, block), lambda j: (0, j)),
        ],
        out_specs=pl.BlockSpec((count, block), lambda j: (0, j)),
        out_shape=jax.ShapeDtypeStruct((count, width), jnp.bfloat16),
        compiler_params=pltpu.CompilerParams(vmem_limit_bytes=32 * MIB),
        cost_estimate=pl.CostEstimate(
            flops=4 * count * features * width,
            bytes_accessed=2 * (count * features + 2 * features * width + count * width),
            transcendentals=count * width,
        ),
    )(rows, gate_cols, up_cols)


def down_kernel(own_ref, mate_ref, own_rows_ref, *refs):
    mate_rows_refs, out_ref = refs[:-1], refs[-1]
    total = jnp.dot(own_ref[...], own_rows_ref[...], preferred_element_type=jnp.float32)
    start = 0
    for rows_ref in mate_rows_refs:
        stop = start + rows_ref.shape[0]
        total = total + jnp.dot(
            mate_ref[:, start:stop], rows_ref[...], preferred_element_type=jnp.float32
        )
        start = stop
    out_ref[...] = total.astype(jnp.bfloat16)


def down(own, mate, own_rows, mate_rows):
    count, depth = own.shape
    width = own_rows.shape[1]
    block = width // 2
    whole = pl.BlockSpec((count, depth), lambda j: (0, 0))
    return pl.pallas_call(
        down_kernel,
        grid=(width // block,),
        in_specs=[whole, whole]
        + [pl.BlockSpec((rows.shape[0], block), lambda j: (0, j)) for rows in (own_rows, *mate_rows)],
        out_specs=pl.BlockSpec((count, block), lambda j: (0, j)),
        out_shape=jax.ShapeDtypeStruct((count, width), jnp.bfloat16),
        compiler_params=pltpu.CompilerParams(vmem_limit_bytes=32 * MIB),
        cost_estimate=pl.CostEstimate(
            flops=4 * count * depth * width,
            bytes_accessed=2 * (2 * count * depth + 2 * depth * width + count * width),
            transcendentals=0,
        ),
    )(own, mate, own_rows, *mate_rows)


def merge_kernel(live_ref, slots_ref, scale_ref, state_ref, returned_ref, out_ref):
    returned = returned_ref[...]
    shape = (state_ref.shape[0], returned.shape[0])
    select = bits(lax.broadcasted_iota(jnp.int32, shape, 1) == slots_ref[...])
    picked = jnp.dot(select, returned, preferred_element_type=jnp.float32)
    old = state_ref[...]
    new = (old.astype(jnp.float32) + scale_ref[...] * picked).astype(jnp.bfloat16)
    out_ref[...] = jnp.where(live_ref[...] > 0, new, old)


def merge(live, slots, scale, state, returned):
    rows, half = state.shape
    count = returned.shape[0]
    return pl.pallas_call(
        merge_kernel,
        out_shape=jax.ShapeDtypeStruct((rows, half), jnp.bfloat16),
        compiler_params=pltpu.CompilerParams(vmem_limit_bytes=32 * MIB),
        cost_estimate=pl.CostEstimate(
            flops=2 * rows * count * half,
            bytes_accessed=2 * (2 * rows + count) * half,
            transcendentals=0,
        ),
    )(live, slots.reshape(rows, 1), scale.reshape(rows, 1), state, returned)


def local(forward_in, reverse_in, w_gate, w_up, w_down, routes, gate_weight):
    sections = lax.axis_size("section")
    lanes = lax.axis_size("expert")
    tick_count = min(2, sections - 1)
    experts = lanes // 2
    token_count, features = forward_in.shape[1:]
    half = features // 2
    most_rows = min(token_count, 3 * token_count // experts)
    slot_total = lanes * most_rows
    position = lax.axis_index("section")
    lane = lax.axis_index("expert")
    side = lane % 2
    group = jnp.where((lane % 4 == 0) | (lane % 4 == 3), 0, 1)
    order = [0, 4, 3, 7, 1, 5, 2, 6]
    members = [2 * e if e % 2 == 0 else 2 * e + 1 for e in order]
    sides = [members, [i ^ 1 for i in members]]
    place = [order.index(e) for e in range(experts)]
    mates = [(i, i ^ 1) for i in range(lanes)]

    def to_mate(array):
        return lax.ppermute(array, "expert", mates)

    def to_section(array, direction, cross):
        by = -1 if direction else 1
        return lax.ppermute(
            array,
            ("section", "expert"),
            [
                (s * lanes + i, (s + by) % sections * lanes + (i ^ cross))
                for s in range(sections)
                for i in range(lanes)
            ],
        )

    def plan(direction, tick):
        batch = (position + (tick if direction else -tick)) % sections
        ids = lax.dynamic_index_in_dim(routes[0, direction, :, :, 0], batch, 0, keepdims=False)
        scale = lax.dynamic_index_in_dim(gate_weight[0, direction], batch, 0, keepdims=False)
        live = (position + tick < sections) if direction else (tick <= position)
        onehot = (ids[:, None] == jnp.arange(experts, dtype=jnp.int32)[None, :]).astype(jnp.int32)
        ranked = (jnp.cumsum(onehot, axis=0) - onehot) * onehot
        start = onehot * (jnp.array(place, jnp.int32) * (2 * most_rows))[None, :]
        return jnp.sum(ranked + start, axis=1), scale, live.astype(jnp.int32).reshape(1, 1)

    plans = [plan(direction, tick) for direction in range(2) for tick in range(tick_count)]
    own_plan = jnp.stack([p[0].astype(jnp.float32) for p in plans] + [p[1] for p in plans])
    mate_plan = to_mate(own_plan)
    own_slots = own_plan[: len(plans)].astype(jnp.int32) + side * most_rows
    mate_slots = mate_plan[: len(plans)].astype(jnp.int32) + (1 - side) * most_rows
    slots = jnp.concatenate([own_slots, mate_slots], axis=1)
    scales = jnp.concatenate([own_plan[len(plans) :], mate_plan[len(plans) :]], axis=1)
    group_flag = group.astype(jnp.int32).reshape(1, 1)

    def pair_slots(direction, tick):
        return slots[direction * tick_count + tick][None]

    gate_cols, up_cols, down_rows = w_gate[0], w_up[0], w_down[0]
    down_own = lax.dynamic_slice_in_dim(down_rows, group * half, half, 1)
    down_other = lax.dynamic_slice_in_dim(down_rows, (1 - group) * half, half, 1)
    depth = down_rows.shape[0] // 2

    def across(array):
        array = array.reshape(experts, 2 * most_rows, array.shape[-1])
        array = lax.all_to_all(array, "expert", 0, 0, axis_index_groups=sides, tiled=True)
        return array.reshape(slot_total, array.shape[-1])

    def expert(received, down_mate):
        active = hidden(received, gate_cols, up_cols)
        return down(active, to_mate(active), down_own, down_mate)

    def near_half(own, mate):
        at = group * half
        return jnp.concatenate(
            [lax.dynamic_slice_in_dim(rows, at, half, 1) for rows in (own, mate)], axis=0
        )

    def finish(direction, tick, near, returned):
        at = direction * tick_count + tick
        return merge(plans[at][2], slots[at], scales[at], near, returned)

    def repack(direction, tick, near, far):
        operands = (group_flag, pair_slots(direction, tick), near, far)
        return pack(pack_kernel, slot_total, features, *operands)

    def result(direction, near):
        own = to_section(near[:token_count], direction, 0)
        mate = to_section(near[token_count:], direction, 1)
        first = group == 0
        return jnp.concatenate(
            [jnp.where(first, own, mate), jnp.where(first, mate, own)], axis=1
        )[None]

    def first_pack(direction, own, mate):
        operands = (pair_slots(direction, 0), own, mate)
        return pack(first_pack_kernel, slot_total, features, *operands)

    forward, reverse = forward_in[0], reverse_in[0]
    forward_mate = to_mate(forward)
    packed_forward = first_pack(0, forward, forward_mate)
    reverse, packed_forward = together(reverse, packed_forward)
    reverse_mate = to_mate(reverse)
    reverse_mate, down_other = together(reverse_mate, down_other)
    down_mate = [to_mate(down_other[:depth])]
    for tick in range(tick_count):
        received = across(packed_forward)
        if tick:
            near = finish(1, tick - 1, reverse_near, returned_reverse)
            reverse_near, reverse_far = to_section(near, 1, 0), to_section(near, 1, 1)
            packed_reverse = repack(1, tick, reverse_near, reverse_far)
        else:
            packed_reverse = first_pack(1, reverse, reverse_mate)
            reverse_near = near_half(reverse, reverse_mate)
            forward_near = near_half(forward, forward_mate)
            packed_reverse, down_mate[0], down_other = together(
                packed_reverse, down_mate[0], down_other
            )
            down_mate.append(to_mate(down_other[depth:]))
        packed_reverse, received = together(packed_reverse, received)
        received_reverse = across(packed_reverse)
        out_forward = expert(received, down_mate)
        out_forward, received_reverse = together(out_forward, received_reverse)
        returned = across(out_forward)
        out_reverse = expert(received_reverse, down_mate)
        out_reverse, returned = together(out_reverse, returned)
        returned_reverse = across(out_reverse)
        near = finish(0, tick, forward_near, returned)
        if tick + 1 < tick_count:
            forward_near, forward_far = to_section(near, 0, 0), to_section(near, 0, 1)
            packed_forward = repack(0, tick + 1, forward_near, forward_far)
            packed_forward, returned_reverse = together(packed_forward, returned_reverse)
        else:
            forward_out = result(0, near)
    reverse_out = result(1, finish(1, tick, reverse_near, returned_reverse))
    return (forward_out, reverse_out)


def solution(mesh):
    return jax.shard_map(
        local,
        mesh=mesh,
        in_specs=(
            P("section", "expert", None),
            P("section", "expert", None),
            P("section", None, "expert"),
            P("section", None, "expert"),
            P("section", "expert", None),
            P("section", None, None, "expert", None),
            P("section", None, None, "expert"),
        ),
        out_specs=(P("section", "expert", None), P("section", "expert", None)),
        check_vma=False,
    )
```

```python
import jax
import jax.numpy as jnp
from jax import lax
from jax.experimental import pallas as pl
from jax.experimental.pallas import tpu as pltpu
from jax.sharding import PartitionSpec as P

epsilon = 1e-06
MIB = 1 << 20


def together(*arrays):
    return lax.optimization_barrier(arrays)


def bits(mask):
    return mask.astype(jnp.float32).astype(jnp.bfloat16)


def normed_select(slots, parts, slot_total):
    widened = [part.astype(jnp.float32) for part in parts]
    total = sum(jnp.sum(part * part, axis=-1, keepdims=True) for part in widened)
    width = sum(part.shape[1] for part in parts)
    inverse = lax.rsqrt(total / width + epsilon)
    select = bits(lax.broadcasted_iota(jnp.int32, (slot_total, slots.shape[1]), 0) == slots)
    packed = []
    for part in widened:
        normed = (part * inverse).astype(jnp.bfloat16)
        rows = jnp.dot(select, normed, preferred_element_type=jnp.float32)
        packed.append(rows.astype(jnp.bfloat16))
    return packed


def first_pack_kernel(slots_ref, own_ref, *refs):
    mate_refs, out_ref = refs[:-1], refs[-1]
    mate = sum(ref[...].astype(jnp.float32) for ref in mate_refs).astype(jnp.bfloat16)
    rows = jnp.concatenate([own_ref[...], mate], axis=0)
    out_ref[...] = normed_select(slots_ref[...], [rows], out_ref.shape[0])[0]


def pack_kernel(group_ref, slots_ref, near_ref, far_ref, out_ref):
    near, far = near_ref[...], far_ref[...]
    half = near.shape[1]
    count = far.shape[0] // 2
    far = jnp.concatenate([far[count:], far[:count]], axis=0)
    first = group_ref[...] == 0
    parts = [jnp.where(first, near, far), jnp.where(first, far, near)]
    low, high = normed_select(slots_ref[...], parts, out_ref.shape[0])
    out_ref[:, :half] = low
    out_ref[:, half:] = high


def pack(kernel, slot_total, features, *operands):
    rows = 128
    return pl.pallas_call(
        kernel,
        out_shape=jax.ShapeDtypeStruct((slot_total, features), jnp.bfloat16),
        compiler_params=pltpu.CompilerParams(vmem_limit_bytes=32 * MIB),
        cost_estimate=pl.CostEstimate(
            flops=2 * slot_total * rows * features,
            bytes_accessed=2 * (slot_total + rows) * features,
            transcendentals=0,
        ),
    )(*operands)


def hidden_kernel(rows_ref, gate_ref, up_ref, out_ref):
    rows = rows_ref[...]
    gate_out = jnp.dot(rows, gate_ref[...], preferred_element_type=jnp.float32)
    up_out = jnp.dot(rows, up_ref[...], preferred_element_type=jnp.float32)
    out_ref[...] = (gate_out / (1.0 + jnp.exp(-gate_out)) * up_out).astype(jnp.bfloat16)


def hidden(rows, gate_cols, up_cols):
    count, features = rows.shape
    width = gate_cols.shape[1]
    block = min(256, width)
    return pl.pallas_call(
        hidden_kernel,
        grid=(width // block,),
        in_specs=[
            pl.BlockSpec((count, features), lambda j: (0, 0)),
            pl.BlockSpec((features, block), lambda j: (0, j)),
            pl.BlockSpec((features, block), lambda j: (0, j)),
        ],
        out_specs=pl.BlockSpec((count, block), lambda j: (0, j)),
        out_shape=jax.ShapeDtypeStruct((count, width), jnp.bfloat16),
        compiler_params=pltpu.CompilerParams(vmem_limit_bytes=56 * MIB),
        cost_estimate=pl.CostEstimate(
            flops=4 * count * features * width,
            bytes_accessed=2 * (count * features + 2 * features * width + count * width),
            transcendentals=count * width,
        ),
    )(rows, gate_cols, up_cols)


def down_kernel(own_ref, mate_ref, own_rows_ref, *refs):
    mate_rows_refs, out_ref = refs[:-1], refs[-1]
    total = jnp.dot(own_ref[...], own_rows_ref[...], preferred_element_type=jnp.float32)
    start = 0
    for rows_ref in mate_rows_refs:
        stop = start + rows_ref.shape[0]
        total = total + jnp.dot(
            mate_ref[:, start:stop], rows_ref[...], preferred_element_type=jnp.float32
        )
        start = stop
    out_ref[...] = total.astype(jnp.bfloat16)


def down(own, mate, own_rows, mate_rows):
    count, depth = own.shape
    width = own_rows.shape[1]
    block = width // 2
    whole = pl.BlockSpec((count, depth), lambda j: (0, 0))
    return pl.pallas_call(
        down_kernel,
        grid=(width // block,),
        in_specs=[whole, whole]
        + [pl.BlockSpec((rows.shape[0], block), lambda j: (0, j)) for rows in (own_rows, *mate_rows)],
        out_specs=pl.BlockSpec((count, block), lambda j: (0, j)),
        out_shape=jax.ShapeDtypeStruct((count, width), jnp.bfloat16),
        compiler_params=pltpu.CompilerParams(vmem_limit_bytes=32 * MIB),
        cost_estimate=pl.CostEstimate(
            flops=4 * count * depth * width,
            bytes_accessed=2 * (2 * count * depth + 2 * depth * width + count * width),
            transcendentals=0,
        ),
    )(own, mate, own_rows, *mate_rows)


def merge_kernel(live_ref, slots_ref, scale_ref, state_ref, returned_ref, out_ref):
    returned = returned_ref[...]
    shape = (state_ref.shape[0], returned.shape[0])
    select = bits(lax.broadcasted_iota(jnp.int32, shape, 1) == slots_ref[...])
    picked = jnp.dot(select, returned, preferred_element_type=jnp.float32)
    old = state_ref[...]
    new = (old.astype(jnp.float32) + scale_ref[...] * picked).astype(jnp.bfloat16)
    out_ref[...] = jnp.where(live_ref[...] > 0, new, old)


def merge(live, slots, scale, state, returned):
    rows, half = state.shape
    count = returned.shape[0]
    return pl.pallas_call(
        merge_kernel,
        out_shape=jax.ShapeDtypeStruct((rows, half), jnp.bfloat16),
        compiler_params=pltpu.CompilerParams(vmem_limit_bytes=32 * MIB),
        cost_estimate=pl.CostEstimate(
            flops=2 * rows * count * half,
            bytes_accessed=2 * (2 * rows + count) * half,
            transcendentals=0,
        ),
    )(live, slots, scale, state, returned)


def local(forward_in, reverse_in, w_gate, w_up, w_down, routes, gate_weight):
    sections = lax.axis_size("section")
    lanes = lax.axis_size("expert")
    tick_count = min(2, sections - 1)
    experts = lanes // 2
    token_count, features = forward_in.shape[1:]
    half = features // 2
    most_rows = min(token_count, 3 * token_count // experts)
    slot_total = lanes * most_rows
    position = lax.axis_index("section")
    lane = lax.axis_index("expert")
    side = lane % 2
    group = jnp.where((lane % 4 == 0) | (lane % 4 == 3), 0, 1)
    order = [0, 2, 4, 6, 5, 7, 1, 3]
    members = [2 * e if e % 2 == 0 else 2 * e + 1 for e in order]
    sides = [members, [i ^ 1 for i in members]]
    place = [order.index(e) for e in range(experts)]
    mates = [(i, i ^ 1) for i in range(lanes)]

    def to_mate(array):
        return lax.ppermute(array, "expert", mates)

    def to_mate_of(array, parity):
        return lax.ppermute(
            array,
            ("section", "expert"),
            [(s * lanes + i, s * lanes + (i ^ 1)) for s in range(parity, sections, 2) for i in range(lanes)],
        )

    def to_section(array, direction, cross):
        by = -1 if direction else 1
        return lax.ppermute(
            array,
            ("section", "expert"),
            [
                (s * lanes + i, (s + by) % sections * lanes + (i ^ cross))
                for s in range(sections)
                for i in range(lanes)
            ],
        )

    def plan(direction, tick):
        batch = (position + (tick if direction else -tick)) % sections
        ids = lax.dynamic_index_in_dim(routes[0, direction, :, :, 0], batch, 0, keepdims=False)
        scale = lax.dynamic_index_in_dim(gate_weight[0, direction], batch, 0, keepdims=False)
        live = (position + tick < sections) if direction else (tick <= position)
        onehot = (ids[:, None] == jnp.arange(experts, dtype=jnp.int32)[None, :]).astype(jnp.int32)
        ranked = (jnp.cumsum(onehot, axis=0) - onehot) * onehot
        start = onehot * (jnp.array(place, jnp.int32) * (2 * most_rows))[None, :]
        return jnp.sum(ranked + start, axis=1), scale, live.astype(jnp.int32).reshape(1, 1)

    plans = [plan(direction, tick) for direction in range(2) for tick in range(tick_count)]
    own_plan = jnp.stack([p[0].astype(jnp.float32) for p in plans] + [p[1] for p in plans])
    mate_plan = to_mate(own_plan)
    late_forward, mate_plan = together(forward_in[0], mate_plan)
    own_slots = own_plan[: len(plans)].astype(jnp.int32) + side * most_rows
    mate_slots = mate_plan[: len(plans)].astype(jnp.int32) + (1 - side) * most_rows
    slots = jnp.concatenate([own_slots, mate_slots], axis=1)
    scales = jnp.concatenate([own_plan[len(plans) :], mate_plan[len(plans) :]], axis=1)
    columns = [
        (slots[at].reshape(-1, 1), scales[at].reshape(-1, 1)) for at in range(len(plans))
    ]
    group_flag = group.astype(jnp.int32).reshape(1, 1)

    def pair_slots(direction, tick):
        return slots[direction * tick_count + tick][None]

    gate_cols, up_cols, down_rows = w_gate[0], w_up[0], w_down[0]
    down_own = lax.dynamic_slice_in_dim(down_rows, group * half, half, 1)
    down_other = lax.dynamic_slice_in_dim(down_rows, (1 - group) * half, half, 1)
    depth = down_rows.shape[0] * 19 // 32

    def across(array):
        array = array.reshape(experts, 2 * most_rows, array.shape[-1])
        array = lax.all_to_all(array, "expert", 0, 0, axis_index_groups=sides, tiled=True)
        return array.reshape(slot_total, array.shape[-1])

    def expert(received, down_mate):
        active = hidden(received, gate_cols, up_cols)
        return down(active, to_mate(active), down_own, down_mate)

    def near_half(own, mate):
        at = group * half
        return jnp.concatenate(
            [lax.dynamic_slice_in_dim(rows, at, half, 1) for rows in (own, mate)], axis=0
        )

    def finish(direction, tick, near, returned):
        at = direction * tick_count + tick
        return merge(plans[at][2], *columns[at], near, returned)

    def repack(direction, tick, near, far):
        operands = (group_flag, pair_slots(direction, tick), near, far)
        return pack(pack_kernel, slot_total, features, *operands)

    def result(direction, near):
        own = to_section(near[:token_count], direction, 0)
        mate = to_section(near[token_count:], direction, 1)
        first = group == 0
        return jnp.concatenate(
            [jnp.where(first, own, mate), jnp.where(first, mate, own)], axis=1
        )[None]

    def first_pack(direction, own, *mate):
        operands = (pair_slots(direction, 0), own, *mate)
        return pack(first_pack_kernel, slot_total, features, *operands)

    forward, reverse = forward_in[0], reverse_in[0]
    forward_mates = [to_mate_of(forward, 1), to_mate_of(late_forward, 0)]
    packed_forward = first_pack(0, forward, *forward_mates)
    forward_mate = forward_mates[0] + forward_mates[1]
    reverse, packed_forward = together(reverse, packed_forward)
    reverse_mate = to_mate(reverse)
    reverse_mate, down_other = together(reverse_mate, down_other)
    down_mate = [to_mate(down_other[:depth])]
    for tick in range(tick_count):
        received = across(packed_forward)
        if tick:
            near = finish(1, tick - 1, reverse_near, returned_reverse)
            reverse_near, reverse_far = to_section(near, 1, 0), to_section(near, 1, 1)
            packed_reverse = repack(1, tick, reverse_near, reverse_far)
        else:
            packed_reverse = first_pack(1, reverse, reverse_mate)
            reverse_near = near_half(reverse, reverse_mate)
            forward_near = near_half(forward, forward_mate)
            packed_reverse, down_mate[0], down_other, forward_near, reverse_near, columns = together(
                packed_reverse, down_mate[0], down_other, forward_near, reverse_near, columns
            )
            down_mate.append(to_mate(down_other[depth:]))
        packed_reverse, received = together(packed_reverse, received)
        received_reverse = across(packed_reverse)
        out_forward = expert(received, down_mate)
        out_forward, received_reverse = together(out_forward, received_reverse)
        returned = across(out_forward)
        out_reverse = expert(received_reverse, down_mate)
        out_reverse, returned = together(out_reverse, returned)
        returned_reverse = across(out_reverse)
        near = finish(0, tick, forward_near, returned)
        if tick + 1 < tick_count:
            forward_near, forward_far = to_section(near, 0, 0), to_section(near, 0, 1)
            packed_forward = repack(0, tick + 1, forward_near, forward_far)
            packed_forward, returned_reverse = together(packed_forward, returned_reverse)
        else:
            forward_out = result(0, near)
    reverse_out = result(1, finish(1, tick, reverse_near, returned_reverse))
    return (forward_out, reverse_out)


def solution(mesh):
    return jax.shard_map(
        local,
        mesh=mesh,
        in_specs=(
            P("section", "expert", None),
            P("section", "expert", None),
            P("section", None, "expert"),
            P("section", None, "expert"),
            P("section", "expert", None),
            P("section", None, None, "expert", None),
            P("section", None, None, "expert"),
        ),
        out_specs=(P("section", "expert", None), P("section", "expert", None)),
        check_vma=False,
    )
```

```python
import jax
import jax.numpy as jnp
from jax import lax
from jax.experimental import pallas as pl
from jax.experimental.pallas import tpu as pltpu
from jax.sharding import PartitionSpec as P

epsilon = 1e-06
MIB = 1 << 20


def together(*arrays):
    return lax.optimization_barrier(arrays)


def bits(mask):
    return mask.astype(jnp.float32).astype(jnp.bfloat16)


def normed_select(slots, parts, slot_total):
    widened = [part.astype(jnp.float32) for part in parts]
    total = sum(jnp.sum(part * part, axis=-1, keepdims=True) for part in widened)
    width = sum(part.shape[1] for part in parts)
    inverse = lax.rsqrt(total / width + epsilon)
    select = bits(lax.broadcasted_iota(jnp.int32, (slot_total, slots.shape[1]), 0) == slots)
    packed = []
    for part in widened:
        normed = (part * inverse).astype(jnp.bfloat16)
        rows = jnp.dot(select, normed, preferred_element_type=jnp.float32)
        packed.append(rows.astype(jnp.bfloat16))
    return packed


def first_pack_kernel(slots_ref, own_ref, *refs):
    mate_refs, out_ref = refs[:-1], refs[-1]
    mate = sum(ref[...].astype(jnp.float32) for ref in mate_refs).astype(jnp.bfloat16)
    rows = jnp.concatenate([own_ref[...], mate], axis=0)
    out_ref[...] = normed_select(slots_ref[...], [rows], out_ref.shape[0])[0]


def pack_kernel(group_ref, slots_ref, near_ref, far_ref, out_ref):
    near, far = near_ref[...], far_ref[...]
    half = near.shape[1]
    count = far.shape[0] // 2
    far = jnp.concatenate([far[count:], far[:count]], axis=0)
    first = group_ref[...] == 0
    parts = [jnp.where(first, near, far), jnp.where(first, far, near)]
    low, high = normed_select(slots_ref[...], parts, out_ref.shape[0])
    out_ref[:, :half] = low
    out_ref[:, half:] = high


def pack(kernel, slot_total, features, *operands):
    rows = 128
    return pl.pallas_call(
        kernel,
        out_shape=jax.ShapeDtypeStruct((slot_total, features), jnp.bfloat16),
        compiler_params=pltpu.CompilerParams(vmem_limit_bytes=32 * MIB),
        cost_estimate=pl.CostEstimate(
            flops=2 * slot_total * rows * features,
            bytes_accessed=2 * (slot_total + rows) * features,
            transcendentals=0,
        ),
    )(*operands)


def hidden_kernel(rows_ref, gate_ref, up_ref, out_ref):
    rows = rows_ref[...]
    gate_out = jnp.dot(rows, gate_ref[...], preferred_element_type=jnp.float32)
    up_out = jnp.dot(rows, up_ref[...], preferred_element_type=jnp.float32)
    out_ref[...] = (gate_out / (1.0 + jnp.exp(-gate_out)) * up_out).astype(jnp.bfloat16)


def hidden(rows, gate_cols, up_cols):
    count, features = rows.shape
    width = gate_cols.shape[1]
    block = min(256, width)
    return pl.pallas_call(
        hidden_kernel,
        grid=(width // block,),
        in_specs=[
            pl.BlockSpec((count, features), lambda j: (0, 0)),
            pl.BlockSpec((features, block), lambda j: (0, j)),
            pl.BlockSpec((features, block), lambda j: (0, j)),
        ],
        out_specs=pl.BlockSpec((count, block), lambda j: (0, j)),
        out_shape=jax.ShapeDtypeStruct((count, width), jnp.bfloat16),
        compiler_params=pltpu.CompilerParams(vmem_limit_bytes=56 * MIB),
        cost_estimate=pl.CostEstimate(
            flops=4 * count * features * width,
            bytes_accessed=2 * (count * features + 2 * features * width + count * width),
            transcendentals=count * width,
        ),
    )(rows, gate_cols, up_cols)


def down_kernel(own_ref, mate_ref, own_rows_ref, *refs):
    mate_rows_refs, out_ref = refs[:-1], refs[-1]
    total = jnp.dot(own_ref[...], own_rows_ref[...], preferred_element_type=jnp.float32)
    start = 0
    for rows_ref in mate_rows_refs:
        stop = start + rows_ref.shape[0]
        total = total + jnp.dot(
            mate_ref[:, start:stop], rows_ref[...], preferred_element_type=jnp.float32
        )
        start = stop
    out_ref[...] = total.astype(jnp.bfloat16)


def down(own, mate, own_rows, mate_rows):
    count, depth = own.shape
    width = own_rows.shape[1]
    block = width // 2
    whole = pl.BlockSpec((count, depth), lambda j: (0, 0))
    return pl.pallas_call(
        down_kernel,
        grid=(width // block,),
        in_specs=[whole, whole]
        + [pl.BlockSpec((rows.shape[0], block), lambda j: (0, j)) for rows in (own_rows, *mate_rows)],
        out_specs=pl.BlockSpec((count, block), lambda j: (0, j)),
        out_shape=jax.ShapeDtypeStruct((count, width), jnp.bfloat16),
        compiler_params=pltpu.CompilerParams(vmem_limit_bytes=32 * MIB),
        cost_estimate=pl.CostEstimate(
            flops=4 * count * depth * width,
            bytes_accessed=2 * (2 * count * depth + 2 * depth * width + count * width),
            transcendentals=0,
        ),
    )(own, mate, own_rows, *mate_rows)


def merge_kernel(live_ref, slots_ref, scale_ref, state_ref, returned_ref, out_ref):
    returned = returned_ref[...]
    shape = (state_ref.shape[0], returned.shape[0])
    select = bits(lax.broadcasted_iota(jnp.int32, shape, 1) == slots_ref[...])
    picked = jnp.dot(select, returned, preferred_element_type=jnp.float32)
    old = state_ref[...]
    new = (old.astype(jnp.float32) + scale_ref[...] * picked).astype(jnp.bfloat16)
    out_ref[...] = jnp.where(live_ref[...] > 0, new, old)


def merge(live, slots, scale, state, returned):
    rows, half = state.shape
    count = returned.shape[0]
    return pl.pallas_call(
        merge_kernel,
        out_shape=jax.ShapeDtypeStruct((rows, half), jnp.bfloat16),
        compiler_params=pltpu.CompilerParams(vmem_limit_bytes=32 * MIB),
        cost_estimate=pl.CostEstimate(
            flops=2 * rows * count * half,
            bytes_accessed=2 * (2 * rows + count) * half,
            transcendentals=0,
        ),
    )(live, slots, scale, state, returned)


def local(forward_in, reverse_in, w_gate, w_up, w_down, routes, gate_weight):
    sections = lax.axis_size("section")
    lanes = lax.axis_size("expert")
    tick_count = min(2, sections - 1)
    experts = lanes // 2
    token_count, features = forward_in.shape[1:]
    half = features // 2
    most_rows = min(token_count, 3 * token_count // experts)
    slot_total = lanes * most_rows
    position = lax.axis_index("section")
    lane = lax.axis_index("expert")
    side = lane % 2
    group = jnp.where((lane % 4 == 0) | (lane % 4 == 3), 0, 1)
    order = [0, 2, 6, 4, 7, 5, 1, 3]
    members = [2 * e if e % 2 == 0 else 2 * e + 1 for e in order]
    sides = [members, [i ^ 1 for i in members]]
    place = [order.index(e) for e in range(experts)]
    mates = [(i, i ^ 1) for i in range(lanes)]

    def to_mate(array):
        return lax.ppermute(array, "expert", mates)

    def to_mate_of(array, parity):
        return lax.ppermute(
            array,
            ("section", "expert"),
            [(s * lanes + i, s * lanes + (i ^ 1)) for s in range(parity, sections, 2) for i in range(lanes)],
        )

    def to_section(array, direction, cross):
        by = -1 if direction else 1
        return lax.ppermute(
            array,
            ("section", "expert"),
            [
                (s * lanes + i, (s + by) % sections * lanes + (i ^ cross))
                for s in range(sections)
                for i in range(lanes)
            ],
        )

    def plan(direction, tick):
        batch = (position + (tick if direction else -tick)) % sections
        ids = lax.dynamic_index_in_dim(routes[0, direction, :, :, 0], batch, 0, keepdims=False)
        scale = lax.dynamic_index_in_dim(gate_weight[0, direction], batch, 0, keepdims=False)
        live = (position + tick < sections) if direction else (tick <= position)
        onehot = (ids[:, None] == jnp.arange(experts, dtype=jnp.int32)[None, :]).astype(jnp.int32)
        ranked = (jnp.cumsum(onehot, axis=0) - onehot) * onehot
        start = onehot * (jnp.array(place, jnp.int32) * (2 * most_rows))[None, :]
        return jnp.sum(ranked + start, axis=1), scale, live.astype(jnp.int32).reshape(1, 1)

    plans = [plan(direction, tick) for direction in range(2) for tick in range(tick_count)]
    own_slots = jnp.stack([p[0] for p in plans])
    mate_slots = to_mate(own_slots)
    late_forward, mate_slots = together(forward_in[0], mate_slots)
    slots = jnp.concatenate(
        [own_slots + side * most_rows, mate_slots + (1 - side) * most_rows], axis=1
    )
    own_scales = jnp.stack([p[1] for p in plans])
    group_flag = group.astype(jnp.int32).reshape(1, 1)

    def pair_slots(direction, tick):
        return slots[direction * tick_count + tick][None]

    gate_cols, up_cols, down_rows = w_gate[0], w_up[0], w_down[0]
    down_own = lax.dynamic_slice_in_dim(down_rows, group * half, half, 1)
    down_other = lax.dynamic_slice_in_dim(down_rows, (1 - group) * half, half, 1)
    depth = down_rows.shape[0] * 19 // 32

    def across(array):
        array = array.reshape(experts, 2 * most_rows, array.shape[-1])
        array = lax.all_to_all(array, "expert", 0, 0, axis_index_groups=sides, tiled=True)
        return array.reshape(slot_total, array.shape[-1])

    def expert(received, down_mate):
        active = hidden(received, gate_cols, up_cols)
        return down(active, to_mate(active), down_own, down_mate)

    def near_half(own, mate):
        at = group * half
        return jnp.concatenate(
            [lax.dynamic_slice_in_dim(rows, at, half, 1) for rows in (own, mate)], axis=0
        )

    def finish(direction, tick, near, returned):
        at = direction * tick_count + tick
        return merge(plans[at][2], *columns[at], near, returned)

    def repack(direction, tick, near, far):
        operands = (group_flag, pair_slots(direction, tick), near, far)
        return pack(pack_kernel, slot_total, features, *operands)

    def result(direction, near):
        own = to_section(near[:token_count], direction, 0)
        mate = to_section(near[token_count:], direction, 1)
        first = group == 0
        return jnp.concatenate(
            [jnp.where(first, own, mate), jnp.where(first, mate, own)], axis=1
        )[None]

    def first_pack(direction, own, *mate):
        operands = (pair_slots(direction, 0), own, *mate)
        return pack(first_pack_kernel, slot_total, features, *operands)

    forward, reverse = forward_in[0], reverse_in[0]
    forward_mates = [to_mate_of(forward, 1), to_mate_of(late_forward, 0)]
    packed_forward = first_pack(0, forward, *forward_mates)
    forward_mate = forward_mates[0] + forward_mates[1]
    reverse, packed_forward, own_scales = together(reverse, packed_forward, own_scales)
    reverse_mate = to_mate(reverse)
    scales = jnp.concatenate([own_scales, to_mate(own_scales)], axis=1)
    columns = [
        (slots[at].reshape(-1, 1), scales[at].reshape(-1, 1)) for at in range(len(plans))
    ]
    reverse_mate, down_other = together(reverse_mate, down_other)
    down_mate = [to_mate(down_other[:depth])]
    for tick in range(tick_count):
        received = across(packed_forward)
        if tick:
            near = finish(1, tick - 1, reverse_near, returned_reverse)
            reverse_near, reverse_far = to_section(near, 1, 0), to_section(near, 1, 1)
            packed_reverse = repack(1, tick, reverse_near, reverse_far)
        else:
            packed_reverse = first_pack(1, reverse, reverse_mate)
            reverse_near = near_half(reverse, reverse_mate)
            forward_near = near_half(forward, forward_mate)
            packed_reverse, down_mate[0], down_other, forward_near, reverse_near, columns = together(
                packed_reverse, down_mate[0], down_other, forward_near, reverse_near, columns
            )
            down_mate.append(to_mate(down_other[depth:]))
        packed_reverse, received = together(packed_reverse, received)
        received_reverse = across(packed_reverse)
        out_forward = expert(received, down_mate)
        out_forward, received_reverse = together(out_forward, received_reverse)
        returned = across(out_forward)
        out_reverse = expert(received_reverse, down_mate)
        out_reverse, returned = together(out_reverse, returned)
        returned_reverse = across(out_reverse)
        near = finish(0, tick, forward_near, returned)
        if tick + 1 < tick_count:
            forward_near, forward_far = to_section(near, 0, 0), to_section(near, 0, 1)
            packed_forward = repack(0, tick + 1, forward_near, forward_far)
            packed_forward, returned_reverse = together(packed_forward, returned_reverse)
        else:
            forward_out = result(0, near)
    reverse_out = result(1, finish(1, tick, reverse_near, returned_reverse))
    return (forward_out, reverse_out)


def solution(mesh):
    return jax.shard_map(
        local,
        mesh=mesh,
        in_specs=(
            P("section", "expert", None),
            P("section", "expert", None),
            P("section", None, "expert"),
            P("section", None, "expert"),
            P("section", "expert", None),
            P("section", None, None, "expert", None),
            P("section", None, None, "expert"),
        ),
        out_specs=(P("section", "expert", None), P("section", "expert", None)),
        check_vma=False,
    )
```

```python
import jax
import jax.numpy as jnp
from jax import lax
from jax.experimental import pallas as pl
from jax.experimental.pallas import tpu as pltpu
from jax.sharding import PartitionSpec as P

epsilon = 1e-06
MIB = 1 << 20


def together(*arrays):
    return lax.optimization_barrier(arrays)


def bits(mask):
    return mask.astype(jnp.float32).astype(jnp.bfloat16)


def normed_select(slots, parts, slot_total):
    widened = [part.astype(jnp.float32) for part in parts]
    total = sum(jnp.sum(part * part, axis=-1, keepdims=True) for part in widened)
    width = sum(part.shape[1] for part in parts)
    inverse = lax.rsqrt(total / width + epsilon)
    select = bits(lax.broadcasted_iota(jnp.int32, (slot_total, slots.shape[1]), 0) == slots)
    packed = []
    for part in widened:
        normed = (part * inverse).astype(jnp.bfloat16)
        rows = jnp.dot(select, normed, preferred_element_type=jnp.float32)
        packed.append(rows.astype(jnp.bfloat16))
    return packed


def first_pack_kernel(slots_ref, own_ref, *refs):
    mate_refs, out_ref = refs[:-1], refs[-1]
    mate = sum(ref[...].astype(jnp.float32) for ref in mate_refs).astype(jnp.bfloat16)
    rows = jnp.concatenate([own_ref[...], mate], axis=0)
    out_ref[...] = normed_select(slots_ref[...], [rows], out_ref.shape[0])[0]


def pack_kernel(group_ref, slots_ref, near_ref, far_ref, out_ref):
    near, far = near_ref[...], far_ref[...]
    half = near.shape[1]
    count = far.shape[0] // 2
    far = jnp.concatenate([far[count:], far[:count]], axis=0)
    first = group_ref[...] == 0
    parts = [jnp.where(first, near, far), jnp.where(first, far, near)]
    low, high = normed_select(slots_ref[...], parts, out_ref.shape[0])
    out_ref[:, :half] = low
    out_ref[:, half:] = high


def pack(kernel, slot_total, features, *operands):
    rows = 128
    return pl.pallas_call(
        kernel,
        out_shape=jax.ShapeDtypeStruct((slot_total, features), jnp.bfloat16),
        compiler_params=pltpu.CompilerParams(vmem_limit_bytes=32 * MIB),
        cost_estimate=pl.CostEstimate(
            flops=2 * slot_total * rows * features,
            bytes_accessed=2 * (slot_total + rows) * features,
            transcendentals=0,
        ),
    )(*operands)


def hidden_kernel(rows_ref, gate_ref, up_ref, out_ref):
    rows = rows_ref[...]
    gate_out = jnp.dot(rows, gate_ref[...], preferred_element_type=jnp.float32)
    up_out = jnp.dot(rows, up_ref[...], preferred_element_type=jnp.float32)
    out_ref[...] = (gate_out / (1.0 + jnp.exp(-gate_out)) * up_out).astype(jnp.bfloat16)


def hidden(rows, gate_cols, up_cols):
    count, features = rows.shape
    width = gate_cols.shape[1]
    block = min(256, width)
    return pl.pallas_call(
        hidden_kernel,
        grid=(width // block,),
        in_specs=[
            pl.BlockSpec((count, features), lambda j: (0, 0)),
            pl.BlockSpec((features, block), lambda j: (0, j)),
            pl.BlockSpec((features, block), lambda j: (0, j)),
        ],
        out_specs=pl.BlockSpec((count, block), lambda j: (0, j)),
        out_shape=jax.ShapeDtypeStruct((count, width), jnp.bfloat16),
        compiler_params=pltpu.CompilerParams(vmem_limit_bytes=56 * MIB),
        cost_estimate=pl.CostEstimate(
            flops=4 * count * features * width,
            bytes_accessed=2 * (count * features + 2 * features * width + count * width),
            transcendentals=count * width,
        ),
    )(rows, gate_cols, up_cols)


def down_kernel(own_ref, mate_ref, own_rows_ref, *refs):
    mate_rows_refs, out_ref = refs[:-1], refs[-1]
    total = jnp.dot(own_ref[...], own_rows_ref[...], preferred_element_type=jnp.float32)
    start = 0
    for rows_ref in mate_rows_refs:
        stop = start + rows_ref.shape[0]
        total = total + jnp.dot(
            mate_ref[:, start:stop], rows_ref[...], preferred_element_type=jnp.float32
        )
        start = stop
    out_ref[...] = total.astype(jnp.bfloat16)


def down(own, mate, own_rows, mate_rows):
    count, depth = own.shape
    width = own_rows.shape[1]
    block = width
    whole = pl.BlockSpec((count, depth), lambda j: (0, 0))
    return pl.pallas_call(
        down_kernel,
        grid=(width // block,),
        in_specs=[whole, whole]
        + [pl.BlockSpec((rows.shape[0], block), lambda j: (0, j)) for rows in (own_rows, *mate_rows)],
        out_specs=pl.BlockSpec((count, block), lambda j: (0, j)),
        out_shape=jax.ShapeDtypeStruct((count, width), jnp.bfloat16),
        compiler_params=pltpu.CompilerParams(vmem_limit_bytes=32 * MIB),
        cost_estimate=pl.CostEstimate(
            flops=4 * count * depth * width,
            bytes_accessed=2 * (2 * count * depth + 2 * depth * width + count * width),
            transcendentals=0,
        ),
    )(own, mate, own_rows, *mate_rows)


def merge_kernel(live_ref, slots_ref, scale_ref, state_ref, returned_ref, out_ref):
    returned = returned_ref[...]
    shape = (state_ref.shape[0], returned.shape[0])
    select = bits(lax.broadcasted_iota(jnp.int32, shape, 1) == slots_ref[...])
    picked = jnp.dot(select, returned, preferred_element_type=jnp.float32)
    old = state_ref[...]
    new = (old.astype(jnp.float32) + scale_ref[...] * picked).astype(jnp.bfloat16)
    out_ref[...] = jnp.where(live_ref[...] > 0, new, old)


def merge(live, slots, scale, state, returned):
    rows, half = state.shape
    count = returned.shape[0]
    return pl.pallas_call(
        merge_kernel,
        out_shape=jax.ShapeDtypeStruct((rows, half), jnp.bfloat16),
        compiler_params=pltpu.CompilerParams(vmem_limit_bytes=32 * MIB),
        cost_estimate=pl.CostEstimate(
            flops=2 * rows * count * half,
            bytes_accessed=2 * (2 * rows + count) * half,
            transcendentals=0,
        ),
    )(live, slots, scale, state, returned)


def local(forward_in, reverse_in, w_gate, w_up, w_down, routes, gate_weight):
    sections = lax.axis_size("section")
    lanes = lax.axis_size("expert")
    tick_count = min(2, sections - 1)
    experts = lanes // 2
    token_count, features = forward_in.shape[1:]
    half = features // 2
    most_rows = min(token_count, 3 * token_count // experts)
    slot_total = lanes * most_rows
    position = lax.axis_index("section")
    lane = lax.axis_index("expert")
    side = lane % 2
    group = jnp.where((lane % 4 == 0) | (lane % 4 == 3), 0, 1)
    order = [0, 2, 6, 4, 7, 5, 1, 3]
    members = [2 * e if e % 2 == 0 else 2 * e + 1 for e in order]
    sides = [members, [i ^ 1 for i in members]]
    place = [order.index(e) for e in range(experts)]
    mates = [(i, i ^ 1) for i in range(lanes)]

    def to_mate(array):
        return lax.ppermute(array, "expert", mates)

    def to_mate_of(array, parity):
        return lax.ppermute(
            array,
            ("section", "expert"),
            [(s * lanes + i, s * lanes + (i ^ 1)) for s in range(parity, sections, 2) for i in range(lanes)],
        )

    def to_section(array, direction, cross):
        by = -1 if direction else 1
        return lax.ppermute(
            array,
            ("section", "expert"),
            [
                (s * lanes + i, (s + by) % sections * lanes + (i ^ cross))
                for s in range(sections)
                for i in range(lanes)
            ],
        )

    def plan(direction, tick):
        batch = (position + (tick if direction else -tick)) % sections
        ids = lax.dynamic_index_in_dim(routes[0, direction, :, :, 0], batch, 0, keepdims=False)
        scale = lax.dynamic_index_in_dim(gate_weight[0, direction], batch, 0, keepdims=False)
        live = (position + tick < sections) if direction else (tick <= position)
        onehot = (ids[:, None] == jnp.arange(experts, dtype=jnp.int32)[None, :]).astype(jnp.int32)
        ranked = (jnp.cumsum(onehot, axis=0) - onehot) * onehot
        start = onehot * (jnp.array(place, jnp.int32) * (2 * most_rows))[None, :]
        return jnp.sum(ranked + start, axis=1), scale, live.astype(jnp.int32).reshape(1, 1)

    plans = [plan(direction, tick) for direction in range(2) for tick in range(tick_count)]
    own_slots = jnp.stack([p[0] for p in plans])
    mate_slots = to_mate(own_slots)
    late_forward, mate_slots = together(forward_in[0], mate_slots)
    slots = jnp.concatenate(
        [own_slots + side * most_rows, mate_slots + (1 - side) * most_rows], axis=1
    )
    own_scales = jnp.stack([p[1] for p in plans])
    group_flag = group.astype(jnp.int32).reshape(1, 1)

    def pair_slots(direction, tick):
        return slots[direction * tick_count + tick][None]

    gate_cols, up_cols, down_rows = w_gate[0], w_up[0], w_down[0]
    down_own = lax.dynamic_slice_in_dim(down_rows, group * half, half, 1)
    down_other = lax.dynamic_slice_in_dim(down_rows, (1 - group) * half, half, 1)
    depth = down_rows.shape[0] * 19 // 32

    def across(array):
        array = array.reshape(experts, 2 * most_rows, array.shape[-1])
        array = lax.all_to_all(array, "expert", 0, 0, axis_index_groups=sides, tiled=True)
        return array.reshape(slot_total, array.shape[-1])

    def expert(received, down_mate):
        active = hidden(received, gate_cols, up_cols)
        return down(active, to_mate(active), down_own, down_mate)

    def near_half(own, mate):
        at = group * half
        return jnp.concatenate(
            [lax.dynamic_slice_in_dim(rows, at, half, 1) for rows in (own, mate)], axis=0
        )

    def finish(direction, tick, near, returned):
        at = direction * tick_count + tick
        return merge(plans[at][2], *columns[at], near, returned)

    def repack(direction, tick, near, far):
        operands = (group_flag, pair_slots(direction, tick), near, far)
        return pack(pack_kernel, slot_total, features, *operands)

    def result(direction, near):
        own = to_section(near[:token_count], direction, 0)
        mate = to_section(near[token_count:], direction, 1)
        first = group == 0
        return jnp.concatenate(
            [jnp.where(first, own, mate), jnp.where(first, mate, own)], axis=1
        )[None]

    def first_pack(direction, own, *mate):
        operands = (pair_slots(direction, 0), own, *mate)
        return pack(first_pack_kernel, slot_total, features, *operands)

    forward, reverse = forward_in[0], reverse_in[0]
    forward_mates = [to_mate_of(forward, 1), to_mate_of(late_forward, 0)]
    packed_forward = first_pack(0, forward, *forward_mates)
    forward_mate = forward_mates[0] + forward_mates[1]
    reverse, packed_forward, own_scales = together(reverse, packed_forward, own_scales)
    reverse_mate = to_mate(reverse)
    scales = jnp.concatenate([own_scales, to_mate(own_scales)], axis=1)
    columns = [
        (slots[at].reshape(-1, 1), scales[at].reshape(-1, 1)) for at in range(len(plans))
    ]
    reverse_mate, down_other = together(reverse_mate, down_other)
    down_mate = [to_mate(down_other[:depth])]
    for tick in range(tick_count):
        received = across(packed_forward)
        if tick:
            near = finish(1, tick - 1, reverse_near, returned_reverse)
            reverse_near, reverse_far = to_section(near, 1, 0), to_section(near, 1, 1)
            packed_reverse = repack(1, tick, reverse_near, reverse_far)
        else:
            packed_reverse = first_pack(1, reverse, reverse_mate)
            reverse_near = near_half(reverse, reverse_mate)
            forward_near = near_half(forward, forward_mate)
            packed_reverse, down_mate[0], down_other, forward_near, reverse_near, columns = together(
                packed_reverse, down_mate[0], down_other, forward_near, reverse_near, columns
            )
            down_mate.append(to_mate(down_other[depth:]))
        packed_reverse, received = together(packed_reverse, received)
        received_reverse = across(packed_reverse)
        out_forward = expert(received, down_mate)
        out_forward, received_reverse = together(out_forward, received_reverse)
        returned = across(out_forward)
        out_reverse = expert(received_reverse, down_mate)
        out_reverse, returned = together(out_reverse, returned)
        returned_reverse = across(out_reverse)
        near = finish(0, tick, forward_near, returned)
        if tick + 1 < tick_count:
            forward_near, forward_far = to_section(near, 0, 0), to_section(near, 0, 1)
            packed_forward = repack(0, tick + 1, forward_near, forward_far)
            packed_forward, returned_reverse = together(packed_forward, returned_reverse)
        else:
            forward_out = result(0, near)
    reverse_out = result(1, finish(1, tick, reverse_near, returned_reverse))
    return (forward_out, reverse_out)


def solution(mesh):
    return jax.shard_map(
        local,
        mesh=mesh,
        in_specs=(
            P("section", "expert", None),
            P("section", "expert", None),
            P("section", None, "expert"),
            P("section", None, "expert"),
            P("section", "expert", None),
            P("section", None, None, "expert", None),
            P("section", None, None, "expert"),
        ),
        out_specs=(P("section", "expert", None), P("section", "expert", None)),
        check_vma=False,
    )
```
